32 devices in a mesh: ctx: 8 (over z, y), grp: 4 (over x, core).
Axes of the slice: x: 2, y: 2, z: 4, core: 2. Of those that a mesh axis runs over, the one named last changes fastest.
Arguments:
- queries: bfloat16 [4, 4096, 512], P('grp', 'ctx'), as said below
- keys: bfloat16 [4, 4096, 512], P('grp', 'ctx'), as said below
- values: bfloat16 [4, 4096, 512], P('grp', 'ctx'), may hold values from -6 to 6
- summary_pos: int32 [4, 8, 8], P('grp', 'ctx'), may hold values from 0 to 511, as said below
Outputs:
- attended: bfloat16 [4, 4096, 512], P('grp', 'ctx')
The draws below stay inside these ranges and needn't reach their ends.
Inputs may be any that keep to these rules, and one draw needn't show every extreme that they name: queries' entries lie within -320 and 320. keys' entries lie within -6 and 6. `summary_pos`: in each block the j-th summary position lies in [j * 64, (j + 1) * 64); the last one is 511.
All inputs are finite; a program needn't handle non-finite values.
Results may differ from the reference program's by a relative error of at most 0.0045.
Values may be sent and summed in bfloat16 or wider, within the bound.
A program may use at most 64 MiB of HBM per device.

```python
import math
import jax
import jax.numpy as jnp
from jax import lax

H = 8
HD = 64
W = 512
BLK = 512
SUMM = 8
NG = 4
ROWB = 8
LCTX = 4096


def shared_keys(key):
    base_keys = jnp.clip(jax.random.normal(jax.random.fold_in(key, 11), (NG, LCTX, W), jnp.float32), -6.0, 6.0)
    return base_keys


def draw_keys(key, part):
    base_keys = shared_keys(key)
    result = base_keys
    return result.astype(jnp.bfloat16)


def draw_queries(key, part):
    noise = 2.0 * jnp.clip(jax.random.normal(jax.random.fold_in(key, 13), (NG, LCTX, W), jnp.float32), -6.0, 6.0)
    result = noise
    return result.astype(jnp.bfloat16)


def draw_summary_pos(key, part):
    spacing = BLK // SUMM
    offsets = jax.random.randint(key, (NG, ROWB, SUMM), 0, spacing, jnp.int32)
    slot_index = jnp.arange(SUMM, dtype=jnp.int32)
    offsets = jnp.where(slot_index[None, None, :] == SUMM - 1, spacing - 1, offsets)
    return (slot_index[None, None, :] * spacing + offsets).astype(jnp.int32)


def steps_of(rng, extent, shards, least, high):
    factor_of = 1.0
    for position, parts in shards:
        steps = jax.random.uniform(jax.random.fold_in(jax.random.fold_in(rng, 6), position), (parts,), jnp.float32, least / len(shards), high / len(shards))
        factor_of = factor_of * jnp.repeat(jnp.exp(steps), extent[position] // parts).reshape((-1,) + (1,) * (len(extent) - 1 - position))
    return factor_of


def bell_draw(stream_key, shape, scale, bound, pieces=(), kind=jnp.bfloat16):
    gain = steps_of(stream_key, shape, pieces, -0.22, 0.18) if pieces else 1.0
    array = jax.random.normal(stream_key, shape, jnp.float32) * scale * gain
    return jnp.minimum(jnp.maximum(array, -bound), bound).astype(kind)


def setup_inputs(seed: int = 0) -> dict:
    arg_keys = jax.random.split(jax.random.key(seed), 5)
    return {
        "queries": draw_queries(jax.random.fold_in(arg_keys[4], 71), 0),
        "keys": draw_keys(jax.random.fold_in(arg_keys[4], 71), 0),
        "values": bell_draw(arg_keys[2], (NG, LCTX, W), 1.0, 6.0, ((0, 4), (1, 8))),
        "summary_pos": draw_summary_pos(jax.random.fold_in(arg_keys[4], 71), 0),
    }


masked_score = -1e+30

def reference(queries, keys, values, summary_pos):
    total_tokens = NG * LCTX
    block_count = total_tokens // BLK
    score_scale = 1.0 / math.sqrt(HD)
    query_all = queries.reshape(total_tokens, H, HD)
    key_all = keys.reshape(total_tokens, H, HD)
    value_all = values.reshape(total_tokens, H, HD)
    positions = summary_pos.reshape(block_count, SUMM)
    picked = (jnp.arange(block_count, dtype=jnp.int32)[:, None] * BLK + positions).reshape(-1).astype(jnp.int32)
    summary_keys = key_all[picked].astype(jnp.float32)
    summary_vals = value_all[picked].astype(jnp.float32)
    summary_block = jnp.repeat(jnp.arange(block_count, dtype=jnp.int32), SUMM)
    padding = jnp.zeros((BLK, H, HD), jnp.bfloat16)
    key_padded = jnp.concatenate([padding, key_all], axis=0)
    value_padded = jnp.concatenate([padding, value_all], axis=0)
    window_index = jnp.arange(2 * BLK, dtype=jnp.int32)
    query_index = jnp.arange(BLK, dtype=jnp.int32)

    def one_block(block):
        start_row = (block * BLK).astype(jnp.int32)
        query_rows = lax.dynamic_slice_in_dim(query_all, start_row, BLK, 0).astype(jnp.float32)
        near_keys = lax.dynamic_slice_in_dim(key_padded, start_row, 2 * BLK, 0).astype(jnp.float32)
        near_vals = lax.dynamic_slice_in_dim(value_padded, start_row, 2 * BLK, 0).astype(jnp.float32)
        near_scores = jnp.einsum('qhd,khd->hqk', query_rows, near_keys) * score_scale
        far_scores = jnp.einsum('qhd,rhd->hqr', query_rows, summary_keys) * score_scale
        own_part = (window_index[None, :] >= BLK) & (window_index[None, :] - BLK <= query_index[:, None])
        prev_part = (window_index[None, :] < BLK) & (block >= 1)
        near_mask = (own_part | prev_part)[None]
        far_mask = (summary_block <= block - 2)[None, None, :]
        near_scores = jnp.where(near_mask, near_scores, masked_score)
        far_scores = jnp.where(far_mask, far_scores, masked_score)
        top_score = jnp.maximum(near_scores.max(-1), far_scores.max(-1))
        near_weight = jnp.where(near_mask, jnp.exp(near_scores - top_score[..., None]), 0.0)
        far_weight = jnp.where(far_mask, jnp.exp(far_scores - top_score[..., None]), 0.0)
        weight_total = near_weight.sum(-1) + far_weight.sum(-1)
        near_low = lax.optimization_barrier(near_weight.astype(jnp.bfloat16)).astype(jnp.float32)
        far_low = lax.optimization_barrier(far_weight.astype(jnp.bfloat16)).astype(jnp.float32)
        numer = jnp.einsum('hqk,khd->qhd', near_low, near_vals) + jnp.einsum('hqr,rhd->qhd', far_low, summary_vals)
        result = numer / jnp.transpose(weight_total)[:, :, None]
        return result.astype(jnp.bfloat16).reshape(BLK, H * HD)
    outputs = lax.map(one_block, jnp.arange(block_count, dtype=jnp.int32))
    return outputs.reshape(NG, LCTX, H * HD)
```

```python
import functools
import math

import jax
import jax.numpy as jnp
from jax import lax
from jax.experimental import pallas as pl
from jax.experimental.pallas import tpu as pltpu
from jax.sharding import PartitionSpec as P

H = 8
HD = 64
BLK = 512
SUMM = 8
PAIR = 2 * HD
SCALE_LOG2E = math.log2(math.e) / math.sqrt(HD)

masked_score = -1e30
MESH = pl.DeviceIdType.MESH


def at(grp, ctx):
    return (ctx, grp)


def scores_of(q, k):
    return lax.dot_general(q, k, (((1,), (1,)), ((), ())), preferred_element_type=jnp.float32)


def kernel(
    ctx_count, grp_count, pos_ref, q_ref, k_ref, v_ref, out_ref,
    prev_k, prev_v, picked, gathered, sum_k, sum_v, peak_ref, acc_ref,
    near_send, near_recv, ctx_send, ctx_recv, grp_send, grp_recv, own_sem,
):
    me_c = lax.axis_index("ctx")
    me_g = lax.axis_index("grp")
    flat = me_g * ctx_count + me_c
    pairs = H // 2
    early = pairs // 2
    half = BLK // 2
    rows_group = ctx_count * 2 * SUMM
    keys_group = ctx_count * SUMM
    at_last = me_c == ctx_count - 1
    has_next = flat < ctx_count * grp_count - 1
    has_prev = flat > 0

    def ctx_peer(step):
        return lax.rem(me_c + step, ctx_count)

    barrier = pltpu.get_barrier_semaphore()
    for step in range(1, ctx_count):
        pl.semaphore_signal(barrier, inc=1, device_id=at(me_g, ctx_peer(step)), device_id_type=MESH)
    for step in range(1, grp_count):
        @pl.when(me_g >= step)
        def _():
            pl.semaphore_signal(barrier, inc=1, device_id=at(lax.rem(me_g - step + grp_count, grp_count), me_c), device_id_type=MESH)

    @pl.when((me_c == 0) & (me_g > 0))
    def _():
        pl.semaphore_signal(
            barrier, inc=1, device_id=at(lax.rem(me_g - 1 + grp_count, grp_count), ctx_count - 1), device_id_type=MESH
        )

    row = lax.broadcasted_iota(jnp.int32, (2 * SUMM, SUMM), 0)
    slot = lax.broadcasted_iota(jnp.int32, (2 * SUMM, SUMM), 1)
    position = pos_ref[...].astype(jnp.float32)
    target = jnp.where((row & (SUMM - 1)) == slot, position, 0.0).sum(-1, keepdims=True)
    column = lax.broadcasted_iota(jnp.int32, (2 * SUMM, BLK), 1)
    choose = jnp.where(column == target.astype(jnp.int32), 1.0, 0.0).astype(jnp.bfloat16)
    chosen_k = jnp.dot(choose, k_ref[...], preferred_element_type=jnp.float32)
    chosen_v = jnp.dot(choose, v_ref[...], preferred_element_type=jnp.float32)
    wide_row = lax.broadcasted_iota(jnp.int32, chosen_k.shape, 0)
    picked[...] = jnp.where(wide_row < SUMM, chosen_k, chosen_v).astype(jnp.bfloat16)

    wraps = jnp.where(at_last & has_next, 1, 0)
    pl.semaphore_wait(barrier, ctx_count - 1 + grp_count - 1 - me_g + wraps)

    def ctx_copy(step):
        return pltpu.make_async_remote_copy(
            src_ref=picked,
            dst_ref=gathered.at[me_g, me_c],
            send_sem=ctx_send.at[step],
            recv_sem=ctx_recv.at[step],
            device_id=at(me_g, ctx_peer(step)),
            device_id_type=MESH,
        )

    def grp_copy(step):
        return pltpu.make_async_remote_copy(
            src_ref=gathered.at[me_g],
            dst_ref=gathered.at[me_g],
            send_sem=grp_send.at[step],
            recv_sem=grp_recv.at[step],
            device_id=at(lax.rem(me_g + step, grp_count), me_c),
            device_id_type=MESH,
        )

    def near_copy(pair, which):
        columns = pl.ds(pair * PAIR, PAIR)
        source, landing = ((k_ref, prev_k), (v_ref, prev_v))[which]
        wrap = lax.div(me_c + 1, ctx_count)
        return pltpu.make_async_remote_copy(
            src_ref=source.at[:, columns],
            dst_ref=landing.at[:, columns],
            send_sem=near_send.at[2 * pair + which],
            recv_sem=near_recv.at[2 * pair + which],
            device_id=at(lax.rem(me_g + wrap, grp_count), ctx_peer(1)),
            device_id_type=MESH,
        )

    for step in range(1, ctx_count):
        ctx_copy(step).start()

    @pl.when(has_next)
    def _():
        for pair in range(pairs):
            near_copy(pair, 0).start()
            near_copy(pair, 1).start()

    own_copy = pltpu.make_async_copy(
        picked,
        gathered.at[me_g, me_c],
        own_sem,
    )
    own_copy.start()

    lane = lax.broadcasted_iota(jnp.int32, (1, PAIR), 1)
    in_head = [
        jnp.where((lane < HD) == (side == 0), 1.0, 0.0).astype(jnp.bfloat16) for side in range(2)
    ]
    off_head = [in_head[1], in_head[0]]

    def weighed(scores, peak, vals, side):
        weights = jnp.exp2((scores - peak) * SCALE_LOG2E).astype(jnp.bfloat16)
        vals_ones = vals * in_head[side] + off_head[side]
        return jnp.dot(weights, vals_ones, preferred_element_type=jnp.float32)

    def fold(head, side, q, keys, vals, allowed):
        scores = scores_of(q * in_head[side], keys)
        if allowed is not None:
            scores = jnp.where(allowed, scores, masked_score)
        old = peak_ref[head][:, :1]
        peak = jnp.maximum(old, scores.max(-1, keepdims=True))
        part = weighed(scores, peak, vals, side)
        rescale = jnp.exp2((old - peak) * SCALE_LOG2E)
        peak_ref[head] = jnp.broadcast_to(peak, (BLK, PAIR))
        return acc_ref[head] * rescale + part

    def columns_of(pair):
        return pl.ds(pair * PAIR, PAIR)

    def own_pair(pair):
        columns = columns_of(pair)
        for side in range(2):
            head = 2 * pair + side
            for part in range(2):
                rows = pl.ds(part * half, half)
                count = (part + 1) * half
                q = q_ref[rows, columns] * in_head[side]
                scores = scores_of(q, k_ref[pl.ds(0, count), columns])
                u = lax.broadcasted_iota(jnp.int32, scores.shape, 1)
                t = lax.broadcasted_iota(jnp.int32, scores.shape, 0) + part * half
                scores = jnp.where(u <= t, scores, masked_score)
                peak = scores.max(-1, keepdims=True)
                acc_ref[head, rows] = weighed(scores, peak, v_ref[pl.ds(0, count), columns], side)
                peak_ref[head, rows] = jnp.broadcast_to(peak, (half, PAIR))

    for pair in range(early):
        own_pair(pair)

    own_copy.wait()
    for step in range(1, ctx_count):
        ctx_copy(step).wait_recv()
    for step in range(1, grp_count):
        @pl.when(me_g + step < grp_count)
        def _():
            grp_copy(step).start()

    for pair in range(early, pairs):
        own_pair(pair)

    for step in range(1, grp_count):
        @pl.when(me_g >= step)
        def _():
            grp_copy(step).wait_recv()

    key_row = lax.broadcasted_iota(jnp.int32, (keys_group, rows_group), 0)
    source_row = lax.broadcasted_iota(jnp.int32, (keys_group, rows_group), 1)
    wanted = key_row * 2 - (key_row & (SUMM - 1))
    take_k = jnp.where(source_row == wanted, 1.0, 0.0).astype(jnp.bfloat16)
    take_v = jnp.where(source_row == wanted + SUMM, 1.0, 0.0).astype(jnp.bfloat16)
    for group in range(grp_count):
        rows = pl.ds(group * keys_group, keys_group)

        @pl.when(me_g >= group)
        def _():
            block = gathered[group].reshape(rows_group, k_ref.shape[1])
            sum_k[rows] = jnp.dot(take_k, block, preferred_element_type=jnp.float32).astype(
                jnp.bfloat16
            )
            sum_v[rows] = jnp.dot(take_v, block, preferred_element_type=jnp.float32).astype(
                jnp.bfloat16
            )

        @pl.when(me_g < group)
        def _():
            sum_k[rows] = jnp.zeros((keys_group, k_ref.shape[1]), jnp.bfloat16)
            sum_v[rows] = jnp.zeros((keys_group, k_ref.shape[1]), jnp.bfloat16)

    summ_rows = grp_count * keys_group
    tile = math.gcd(summ_rows, BLK)

    def far_pair(pair):
        columns = columns_of(pair)

        def far_tile(index, inner):
            rows = pl.ds(index * tile, tile)
            key_index = lax.broadcasted_iota(jnp.int32, (1, tile), 1) + index * tile
            allowed = key_index < (flat - 1) * SUMM
            for side in range(2):
                head = 2 * pair + side
                acc_ref[head] = fold(
                    head, side, q_ref[:, columns], sum_k[rows, columns], sum_v[rows, columns],
                    allowed,
                )
            return inner

        if summ_rows == tile:
            return far_tile(0, None)
        return lax.fori_loop(0, summ_rows // tile, far_tile, None)

    for pair in range(pairs):
        far_pair(pair)

    def near_pair(pair):
        columns = columns_of(pair)

        @pl.when(has_prev)
        def _():
            near_copy(pair, 0).wait_recv()
            near_copy(pair, 1).wait_recv()
            for side in range(2):
                head = 2 * pair + side
                acc_ref[head] = fold(
                    head, side, q_ref[:, columns], prev_k[:, columns], prev_v[:, columns], None
                )

        even, odd = acc_ref[2 * pair], acc_ref[2 * pair + 1]
        first = lane < HD
        numer = jnp.where(first, even, odd)
        total = pltpu.roll(jnp.where(first, odd, even), HD, 1)
        out_ref[:, columns] = (numer / total).astype(jnp.bfloat16)

    for pair in range(pairs):
        near_pair(pair)

    for step in range(1, ctx_count):
        ctx_copy(step).wait_send()
    for step in range(1, grp_count):
        @pl.when(me_g + step < grp_count)
        def _():
            grp_copy(step).wait_send()

    @pl.when(has_next)
    def _():
        for pair in range(pairs):
            near_copy(pair, 0).wait_send()
            near_copy(pair, 1).wait_send()


def shards(queries, keys, values, summary_pos):
    ctx_count = lax.axis_size("ctx")
    grp_count = lax.axis_size("grp")
    unused, tokens, width = queries.shape
    assert tokens == BLK and width == H * HD
    pairs = H // 2
    group_keys = ctx_count * SUMM
    all_keys = grp_count * group_keys
    vmem = pl.BlockSpec(memory_space=pltpu.VMEM)
    return pl.pallas_call(
        functools.partial(kernel, ctx_count, grp_count),
        out_shape=jax.ShapeDtypeStruct((tokens, width), jnp.bfloat16),
        in_specs=[vmem, vmem, vmem, vmem],
        out_specs=vmem,
        scratch_shapes=[
            pltpu.VMEM((tokens, width), jnp.bfloat16),
            pltpu.VMEM((tokens, width), jnp.bfloat16),
            pltpu.VMEM((2 * SUMM, width), jnp.bfloat16),
            pltpu.VMEM((grp_count, ctx_count, 2 * SUMM, width), jnp.bfloat16),
            pltpu.VMEM((all_keys, width), jnp.bfloat16),
            pltpu.VMEM((all_keys, width), jnp.bfloat16),
            pltpu.VMEM((H, tokens, PAIR), jnp.float32),
            pltpu.VMEM((H, tokens, PAIR), jnp.float32),
            pltpu.SemaphoreType.DMA((2 * pairs,)),
            pltpu.SemaphoreType.DMA((2 * pairs,)),
            pltpu.SemaphoreType.DMA((ctx_count,)),
            pltpu.SemaphoreType.DMA((ctx_count,)),
            pltpu.SemaphoreType.DMA((grp_count,)),
            pltpu.SemaphoreType.DMA((grp_count,)),
            pltpu.SemaphoreType.DMA,
        ],
        compiler_params=pltpu.CompilerParams(
            collective_id=0, has_side_effects=True, vmem_limit_bytes=48 * 1024 * 1024
        ),
    )(summary_pos[0], queries[0], keys[0], values[0])[None]


def solution(mesh):
    placed = (
        P("grp", "ctx", None),
        P("grp", "ctx", None),
        P("grp", "ctx", None),
        P("grp", "ctx", None),
    )
    return jax.shard_map(
        shards, mesh=mesh, in_specs=placed, out_specs=P("grp", "ctx", None), check_vma=False
    )
```

```python
import functools
import math

import jax
import jax.numpy as jnp
from jax import lax
from jax.experimental import pallas as pl
from jax.experimental.pallas import tpu as pltpu
from jax.sharding import PartitionSpec as P

H = 8
HD = 64
BLK = 512
SUMM = 8
PAIR = 2 * HD
SCALE_LOG2E = math.log2(math.e) / math.sqrt(HD)

masked_score = -1e30
MESH = pl.DeviceIdType.MESH


def at(grp, ctx):
    return (ctx, grp)


def scores_of(q, k):
    return lax.dot_general(q, k, (((1,), (1,)), ((), ())), preferred_element_type=jnp.float32)


def kernel(
    ctx_count, grp_count, pos_in, q_in, k_in, v_in, out_ref,
    pos_ref, q_ref, k_ref, v_ref, prev_k, prev_v, picked, gathered, sum_k, sum_v, peak_ref, acc_ref,
    near_send, near_recv, ctx_send, ctx_recv, grp_send, grp_recv, own_sem, load_sem,
):
    me_c = lax.axis_index("ctx")
    me_g = lax.axis_index("grp")
    flat = me_g * ctx_count + me_c
    pairs = H // 2
    early = 1
    ahead = 2
    half = BLK // 2
    rows_group = ctx_count * 2 * SUMM
    keys_group = ctx_count * SUMM
    at_last = me_c == ctx_count - 1
    has_next = flat < ctx_count * grp_count - 1
    has_prev = flat > 0

    def ctx_peer(step):
        return lax.rem(me_c + step, ctx_count)

    loads = [
        pltpu.make_async_copy(source, landing, load_sem.at[number])
        for number, (source, landing) in enumerate(
            ((pos_in, pos_ref), (k_in, k_ref), (v_in, v_ref), (q_in, q_ref))
        )
    ]
    for load in loads:
        load.start()

    barrier = pltpu.get_barrier_semaphore()
    for step in range(1, ctx_count):
        pl.semaphore_signal(barrier, inc=1, device_id=at(me_g, ctx_peer(step)), device_id_type=MESH)
    for step in range(1, grp_count):
        @pl.when(me_g >= step)
        def _():
            pl.semaphore_signal(barrier, inc=1, device_id=at(lax.rem(me_g - step + grp_count, grp_count), me_c), device_id_type=MESH)

    @pl.when((me_c == 0) & (me_g > 0))
    def _():
        pl.semaphore_signal(
            barrier, inc=1, device_id=at(lax.rem(me_g - 1 + grp_count, grp_count), ctx_count - 1), device_id_type=MESH
        )

    for load in loads[:3]:
        load.wait()
    row = lax.broadcasted_iota(jnp.int32, (2 * SUMM, SUMM), 0)
    slot = lax.broadcasted_iota(jnp.int32, (2 * SUMM, SUMM), 1)
    position = pos_ref[...].astype(jnp.float32)
    target = jnp.where((row & (SUMM - 1)) == slot, position, 0.0).sum(-1, keepdims=True)
    column = lax.broadcasted_iota(jnp.int32, (2 * SUMM, BLK), 1)
    choose = jnp.where(column == target.astype(jnp.int32), 1.0, 0.0).astype(jnp.bfloat16)
    chosen_k = jnp.dot(choose, k_ref[...], preferred_element_type=jnp.float32)
    chosen_v = jnp.dot(choose, v_ref[...], preferred_element_type=jnp.float32)
    wide_row = lax.broadcasted_iota(jnp.int32, chosen_k.shape, 0)
    picked[...] = jnp.where(wide_row < SUMM, chosen_k, chosen_v).astype(jnp.bfloat16)

    wraps = jnp.where(at_last & has_next, 1, 0)
    pl.semaphore_wait(barrier, ctx_count - 1 + grp_count - 1 - me_g + wraps)

    def ctx_copy(step):
        return pltpu.make_async_remote_copy(
            src_ref=picked,
            dst_ref=gathered.at[me_g, me_c],
            send_sem=ctx_send.at[step],
            recv_sem=ctx_recv.at[step],
            device_id=at(me_g, ctx_peer(step)),
            device_id_type=MESH,
        )

    def grp_copy(step):
        return pltpu.make_async_remote_copy(
            src_ref=gathered.at[me_g],
            dst_ref=gathered.at[me_g],
            send_sem=grp_send.at[step],
            recv_sem=grp_recv.at[step],
            device_id=at(lax.rem(me_g + step, grp_count), me_c),
            device_id_type=MESH,
        )

    def near_copy(pair, which):
        columns = pl.ds(pair * PAIR, PAIR)
        source, landing = ((k_in, prev_k), (v_in, prev_v))[which]
        wrap = lax.div(me_c + 1, ctx_count)
        return pltpu.make_async_remote_copy(
            src_ref=source.at[:, columns],
            dst_ref=landing.at[:, columns],
            send_sem=near_send.at[2 * pair + which],
            recv_sem=near_recv.at[2 * pair + which],
            device_id=at(lax.rem(me_g + wrap, grp_count), ctx_peer(1)),
            device_id_type=MESH,
        )

    for step in range(1, ctx_count):
        ctx_copy(step).start()

    def near_start(pair):
        near_copy(pair, 0).start()
        near_copy(pair, 1).start()

    @pl.when(has_next & ~at_last)
    def _():
        for pair in range(ahead):
            near_start(pair)

    own_copy = pltpu.make_async_copy(
        picked,
        gathered.at[me_g, me_c],
        own_sem,
    )
    own_copy.start()
    loads[3].wait()

    lane = lax.broadcasted_iota(jnp.int32, (1, PAIR), 1)
    in_head = [
        jnp.where((lane < HD) == (side == 0), 1.0, 0.0).astype(jnp.bfloat16) for side in range(2)
    ]
    off_head = [in_head[1], in_head[0]]

    def weighed(scores, peak, vals, side):
        weights = jnp.exp2((scores - peak) * SCALE_LOG2E).astype(jnp.bfloat16)
        vals_ones = vals * in_head[side] + off_head[side]
        return jnp.dot(weights, vals_ones, preferred_element_type=jnp.float32)

    def fold(head, side, q, keys, vals, allowed):
        scores = scores_of(q * in_head[side], keys)
        if allowed is not None:
            scores = jnp.where(allowed, scores, masked_score)
        old = peak_ref[head][:, :1]
        peak = jnp.maximum(old, scores.max(-1, keepdims=True))
        part = weighed(scores, peak, vals, side)
        rescale = jnp.exp2((old - peak) * SCALE_LOG2E)
        peak_ref[head] = jnp.broadcast_to(peak, (BLK, PAIR))
        return acc_ref[head] * rescale + part

    def columns_of(pair):
        return pl.ds(pair * PAIR, PAIR)

    def own_pair(pair):
        columns = columns_of(pair)
        for side in range(2):
            head = 2 * pair + side
            for part in range(2):
                rows = pl.ds(part * half, half)
                count = (part + 1) * half
                q = q_ref[rows, columns] * in_head[side]
                scores = scores_of(q, k_ref[pl.ds(0, count), columns])
                u = lax.broadcasted_iota(jnp.int32, scores.shape, 1)
                t = lax.broadcasted_iota(jnp.int32, scores.shape, 0) + part * half
                scores = jnp.where(u <= t, scores, masked_score)
                peak = scores.max(-1, keepdims=True)
                acc_ref[head, rows] = weighed(scores, peak, v_ref[pl.ds(0, count), columns], side)
                peak_ref[head, rows] = jnp.broadcast_to(peak, (half, PAIR))

    for pair in range(early):
        own_pair(pair)

    own_copy.wait()
    for step in range(1, ctx_count):
        ctx_copy(step).wait_recv()

    @pl.when(has_next & at_last)
    def _():
        for pair in range(ahead):
            near_start(pair)

    for step in range(1, grp_count):
        @pl.when(me_g + step < grp_count)
        def _():
            grp_copy(step).start()

    for pair in range(early, pairs):
        own_pair(pair)

    for step in range(1, grp_count):
        @pl.when(me_g >= step)
        def _():
            grp_copy(step).wait_recv()

    key_row = lax.broadcasted_iota(jnp.int32, (keys_group, rows_group), 0)
    source_row = lax.broadcasted_iota(jnp.int32, (keys_group, rows_group), 1)
    wanted = key_row * 2 - (key_row & (SUMM - 1))
    take_k = jnp.where(source_row == wanted, 1.0, 0.0).astype(jnp.bfloat16)
    take_v = jnp.where(source_row == wanted + SUMM, 1.0, 0.0).astype(jnp.bfloat16)
    for group in range(grp_count):
        rows = pl.ds(group * keys_group, keys_group)

        @pl.when(me_g >= group)
        def _():
            block = gathered[group].reshape(rows_group, k_ref.shape[1])
            sum_k[rows] = jnp.dot(take_k, block, preferred_element_type=jnp.float32).astype(
                jnp.bfloat16
            )
            sum_v[rows] = jnp.dot(take_v, block, preferred_element_type=jnp.float32).astype(
                jnp.bfloat16
            )

        @pl.when(me_g < group)
        def _():
            sum_k[rows] = jnp.zeros((keys_group, k_ref.shape[1]), jnp.bfloat16)
            sum_v[rows] = jnp.zeros((keys_group, k_ref.shape[1]), jnp.bfloat16)

    summ_rows = grp_count * keys_group
    tile = math.gcd(summ_rows, BLK)

    def far_pair(pair):
        columns = columns_of(pair)

        def far_tile(index, inner):
            rows = pl.ds(index * tile, tile)
            key_index = lax.broadcasted_iota(jnp.int32, (1, tile), 1) + index * tile
            allowed = key_index < (flat - 1) * SUMM
            for side in range(2):
                head = 2 * pair + side
                acc_ref[head] = fold(
                    head, side, q_ref[:, columns], sum_k[rows, columns], sum_v[rows, columns],
                    allowed,
                )
            return inner

        if summ_rows == tile:
            return far_tile(0, None)
        return lax.fori_loop(0, summ_rows // tile, far_tile, None)

    for pair in range(pairs):
        far_pair(pair)

    def near_pair(pair):
        columns = columns_of(pair)

        @pl.when(has_next)
        def _():
            near_copy(pair, 0).wait_send()
            near_copy(pair, 1).wait_send()
            if pair + ahead < pairs:
                near_start(pair + ahead)

        @pl.when(has_prev)
        def _():
            near_copy(pair, 0).wait_recv()
            near_copy(pair, 1).wait_recv()
            for side in range(2):
                head = 2 * pair + side
                acc_ref[head] = fold(
                    head, side, q_ref[:, columns], prev_k[:, columns], prev_v[:, columns], None
                )

        even, odd = acc_ref[2 * pair], acc_ref[2 * pair + 1]
        first = lane < HD
        numer = jnp.where(first, even, odd)
        total = pltpu.roll(jnp.where(first, odd, even), HD, 1)
        out_ref[:, columns] = (numer / total).astype(jnp.bfloat16)

    for pair in range(pairs):
        near_pair(pair)

    for step in range(1, ctx_count):
        ctx_copy(step).wait_send()
    for step in range(1, grp_count):
        @pl.when(me_g + step < grp_count)
        def _():
            grp_copy(step).wait_send()


def shards(queries, keys, values, summary_pos):
    ctx_count = lax.axis_size("ctx")
    grp_count = lax.axis_size("grp")
    unused, tokens, width = queries.shape
    assert tokens == BLK and width == H * HD
    pairs = H // 2
    group_keys = ctx_count * SUMM
    all_keys = grp_count * group_keys
    vmem = pl.BlockSpec(memory_space=pltpu.VMEM)
    return pl.pallas_call(
        functools.partial(kernel, ctx_count, grp_count),
        out_shape=jax.ShapeDtypeStruct((tokens, width), jnp.bfloat16),
        in_specs=[pl.BlockSpec(memory_space=pl.ANY)] * 4,
        out_specs=vmem,
        scratch_shapes=[
            pltpu.VMEM((1, SUMM), jnp.int32),
            pltpu.VMEM((tokens, width), jnp.bfloat16),
            pltpu.VMEM((tokens, width), jnp.bfloat16),
            pltpu.VMEM((tokens, width), jnp.bfloat16),
            pltpu.VMEM((tokens, width), jnp.bfloat16),
            pltpu.VMEM((tokens, width), jnp.bfloat16),
            pltpu.VMEM((2 * SUMM, width), jnp.bfloat16),
            pltpu.VMEM((grp_count, ctx_count, 2 * SUMM, width), jnp.bfloat16),
            pltpu.VMEM((all_keys, width), jnp.bfloat16),
            pltpu.VMEM((all_keys, width), jnp.bfloat16),
            pltpu.VMEM((H, tokens, PAIR), jnp.float32),
            pltpu.VMEM((H, tokens, PAIR), jnp.float32),
            pltpu.SemaphoreType.DMA((2 * pairs,)),
            pltpu.SemaphoreType.DMA((2 * pairs,)),
            pltpu.SemaphoreType.DMA((ctx_count,)),
            pltpu.SemaphoreType.DMA((ctx_count,)),
            pltpu.SemaphoreType.DMA((grp_count,)),
            pltpu.SemaphoreType.DMA((grp_count,)),
            pltpu.SemaphoreType.DMA,
            pltpu.SemaphoreType.DMA((4,)),
        ],
        compiler_params=pltpu.CompilerParams(
            collective_id=0, has_side_effects=True, vmem_limit_bytes=56 * 1024 * 1024
        ),
    )(summary_pos[0], queries[0], keys[0], values[0])[None]


def solution(mesh):
    placed = (
        P("grp", "ctx", None),
        P("grp", "ctx", None),
        P("grp", "ctx", None),
        P("grp", "ctx", None),
    )
    return jax.shard_map(
        shards, mesh=mesh, in_specs=placed, out_specs=P("grp", "ctx", None), check_vma=False
    )
```

```python
import functools
import math

import jax
import jax.numpy as jnp
from jax import lax
from jax.experimental import pallas as pl
from jax.experimental.pallas import tpu as pltpu
from jax.sharding import PartitionSpec as P

H = 8
HD = 64
BLK = 512
SUMM = 8
PAIR = 2 * HD
SCALE_LOG2E = math.log2(math.e) / math.sqrt(HD)

masked_score = -1e30
MESH = pl.DeviceIdType.MESH


def at(grp, ctx):
    return (ctx, grp)


def scores_of(q, k):
    return lax.dot_general(q, k, (((1,), (1,)), ((), ())), preferred_element_type=jnp.float32)


def kernel(
    ctx_count, grp_count, pos_in, q_in, k_in, v_in, out_ref,
    pos_ref, q_ref, k_ref, v_ref, prev_k, prev_v, picked, gathered, sum_k, sum_v, peak_ref, acc_ref,
    near_send, near_recv, ctx_send, ctx_recv, grp_send, grp_recv, own_sem, load_sem,
):
    me_c = lax.axis_index("ctx")
    me_g = lax.axis_index("grp")
    flat = me_g * ctx_count + me_c
    pairs = H // 2
    early = 1
    ahead = pairs - 1
    half = BLK // 2
    rows_group = ctx_count * 2 * SUMM
    keys_group = ctx_count * SUMM
    at_last = me_c == ctx_count - 1
    has_next = flat < ctx_count * grp_count - 1
    has_prev = flat > 0

    def ctx_peer(step):
        return lax.rem(me_c + step, ctx_count)

    loads = [
        pltpu.make_async_copy(source, landing, load_sem.at[number])
        for number, (source, landing) in enumerate(
            ((pos_in, pos_ref), (k_in, k_ref), (v_in, v_ref), (q_in, q_ref))
        )
    ]
    for load in loads:
        load.start()

    barrier = pltpu.get_barrier_semaphore()
    for step in range(1, ctx_count):
        pl.semaphore_signal(barrier, inc=1, device_id=at(me_g, ctx_peer(step)), device_id_type=MESH)
    for step in range(1, grp_count):
        @pl.when(me_g >= step)
        def _():
            pl.semaphore_signal(barrier, inc=1, device_id=at(lax.rem(me_g - step + grp_count, grp_count), me_c), device_id_type=MESH)

    @pl.when((me_c == 0) & (me_g > 0))
    def _():
        pl.semaphore_signal(
            barrier, inc=1, device_id=at(lax.rem(me_g - 1 + grp_count, grp_count), ctx_count - 1), device_id_type=MESH
        )

    for load in loads[:3]:
        load.wait()
    row = lax.broadcasted_iota(jnp.int32, (2 * SUMM, SUMM), 0)
    slot = lax.broadcasted_iota(jnp.int32, (2 * SUMM, SUMM), 1)
    position = pos_ref[...].astype(jnp.float32)
    target = jnp.where((row & (SUMM - 1)) == slot, position, 0.0).sum(-1, keepdims=True)
    column = lax.broadcasted_iota(jnp.int32, (2 * SUMM, BLK), 1)
    choose = jnp.where(column == target.astype(jnp.int32), 1.0, 0.0).astype(jnp.bfloat16)
    chosen_k = jnp.dot(choose, k_ref[...], preferred_element_type=jnp.float32)
    chosen_v = jnp.dot(choose, v_ref[...], preferred_element_type=jnp.float32)
    wide_row = lax.broadcasted_iota(jnp.int32, chosen_k.shape, 0)
    picked[...] = jnp.where(wide_row < SUMM, chosen_k, chosen_v).astype(jnp.bfloat16)

    wraps = jnp.where(at_last & has_next, 1, 0)
    pl.semaphore_wait(barrier, ctx_count - 1 + grp_count - 1 - me_g + wraps)

    def ctx_copy(step):
        return pltpu.make_async_remote_copy(
            src_ref=picked,
            dst_ref=gathered.at[me_g, me_c],
            send_sem=ctx_send.at[step],
            recv_sem=ctx_recv.at[step],
            device_id=at(me_g, ctx_peer(step)),
            device_id_type=MESH,
        )

    def grp_copy(step):
        return pltpu.make_async_remote_copy(
            src_ref=gathered.at[me_g],
            dst_ref=gathered.at[me_g],
            send_sem=grp_send.at[step],
            recv_sem=grp_recv.at[step],
            device_id=at(lax.rem(me_g + step, grp_count), me_c),
            device_id_type=MESH,
        )

    def near_copy(pair, which):
        columns = pl.ds(pair * PAIR, PAIR)
        source, landing = ((k_in, prev_k), (v_in, prev_v))[which]
        wrap = lax.div(me_c + 1, ctx_count)
        return pltpu.make_async_remote_copy(
            src_ref=source.at[:, columns],
            dst_ref=landing.at[:, columns],
            send_sem=near_send.at[2 * pair + which],
            recv_sem=near_recv.at[2 * pair + which],
            device_id=at(lax.rem(me_g + wrap, grp_count), ctx_peer(1)),
            device_id_type=MESH,
        )

    for step in range(1, ctx_count):
        ctx_copy(step).start()

    def near_start(pair):
        near_copy(pair, 0).start()
        near_copy(pair, 1).start()

    def near_wait_send(pair):
        near_copy(pair, 0).wait_send()
        near_copy(pair, 1).wait_send()

    @pl.when(has_next & ~at_last)
    def _():
        for pair in range(ahead):
            near_start(pair)

    own_copy = pltpu.make_async_copy(
        picked,
        gathered.at[me_g, me_c],
        own_sem,
    )
    own_copy.start()
    loads[3].wait()

    lane = lax.broadcasted_iota(jnp.int32, (1, PAIR), 1)
    in_head = [
        jnp.where((lane < HD) == (side == 0), 1.0, 0.0).astype(jnp.bfloat16) for side in range(2)
    ]
    off_head = [in_head[1], in_head[0]]

    def weighed(scores, peak, vals, side):
        weights = jnp.exp2((scores - peak) * SCALE_LOG2E).astype(jnp.bfloat16)
        vals_ones = vals * in_head[side] + off_head[side]
        return jnp.dot(weights, vals_ones, preferred_element_type=jnp.float32)

    def fold(head, side, q, keys, vals, allowed):
        scores = scores_of(q * in_head[side], keys)
        if allowed is not None:
            scores = jnp.where(allowed, scores, masked_score)
        old = peak_ref[head][:, :1]
        peak = jnp.maximum(old, scores.max(-1, keepdims=True))
        part = weighed(scores, peak, vals, side)
        rescale = jnp.exp2((old - peak) * SCALE_LOG2E)
        peak_ref[head] = jnp.broadcast_to(peak, (BLK, PAIR))
        return acc_ref[head] * rescale + part

    def columns_of(pair):
        return pl.ds(pair * PAIR, PAIR)

    def own_pair(pair):
        columns = columns_of(pair)
        for side in range(2):
            head = 2 * pair + side
            for part in range(2):
                rows = pl.ds(part * half, half)
                count = (part + 1) * half
                q = q_ref[rows, columns] * in_head[side]
                scores = scores_of(q, k_ref[pl.ds(0, count), columns])
                u = lax.broadcasted_iota(jnp.int32, scores.shape, 1)
                t = lax.broadcasted_iota(jnp.int32, scores.shape, 0) + part * half
                scores = jnp.where(u <= t, scores, masked_score)
                peak = scores.max(-1, keepdims=True)
                acc_ref[head, rows] = weighed(scores, peak, v_ref[pl.ds(0, count), columns], side)
                peak_ref[head, rows] = jnp.broadcast_to(peak, (half, PAIR))

    for pair in range(early):
        own_pair(pair)

    own_copy.wait()
    for step in range(1, ctx_count):
        ctx_copy(step).wait_recv()

    @pl.when(has_next & at_last)
    def _():
        for pair in range(ahead):
            near_start(pair)

    for step in range(1, grp_count):
        @pl.when(me_g + step < grp_count)
        def _():
            grp_copy(step).start()

    for pair in range(early, pairs):
        own_pair(pair)

    key_row = lax.broadcasted_iota(jnp.int32, (keys_group, rows_group), 0)
    source_row = lax.broadcasted_iota(jnp.int32, (keys_group, rows_group), 1)
    wanted = key_row * 2 - (key_row & (SUMM - 1))
    take_k = jnp.where(source_row == wanted, 1.0, 0.0).astype(jnp.bfloat16)
    take_v = jnp.where(source_row == wanted + SUMM, 1.0, 0.0).astype(jnp.bfloat16)
    def take_summaries():
        for step in range(1, grp_count):
            @pl.when(me_g >= step)
            def _():
                grp_copy(step).wait_recv()

        for group in range(grp_count):
            rows = pl.ds(group * keys_group, keys_group)

            @pl.when(me_g >= group)
            def _():
                block = gathered[group].reshape(rows_group, k_ref.shape[1])
                sum_k[rows] = jnp.dot(take_k, block, preferred_element_type=jnp.float32).astype(
                    jnp.bfloat16
                )
                sum_v[rows] = jnp.dot(take_v, block, preferred_element_type=jnp.float32).astype(
                    jnp.bfloat16
                )

            @pl.when(me_g < group)
            def _():
                sum_k[rows] = jnp.zeros((keys_group, k_ref.shape[1]), jnp.bfloat16)
                sum_v[rows] = jnp.zeros((keys_group, k_ref.shape[1]), jnp.bfloat16)

    summ_rows = grp_count * keys_group
    tile = math.gcd(summ_rows, BLK)

    def far_pair(pair):
        columns = columns_of(pair)

        def far_tile(index, inner):
            rows = pl.ds(index * tile, tile)
            key_index = lax.broadcasted_iota(jnp.int32, (1, tile), 1) + index * tile
            allowed = key_index < (flat - 1) * SUMM
            for side in range(2):
                head = 2 * pair + side
                acc_ref[head] = fold(
                    head, side, q_ref[:, columns], sum_k[rows, columns], sum_v[rows, columns],
                    allowed,
                )
            return inner

        if summ_rows == tile:
            return far_tile(0, None)
        return lax.fori_loop(0, summ_rows // tile, far_tile, None)

    def near_pair(pair):
        columns = columns_of(pair)

        if pair + ahead < pairs:
            @pl.when(has_next)
            def _():
                near_wait_send(pair)
                near_start(pair + ahead)

        @pl.when(has_prev)
        def _():
            near_copy(pair, 0).wait_recv()
            near_copy(pair, 1).wait_recv()
            for side in range(2):
                head = 2 * pair + side
                acc_ref[head] = fold(
                    head, side, q_ref[:, columns], prev_k[:, columns], prev_v[:, columns], None
                )

    def finish_pair(pair):
        columns = columns_of(pair)
        even, odd = acc_ref[2 * pair], acc_ref[2 * pair + 1]
        first = lane < HD
        numer = jnp.where(first, even, odd)
        total = pltpu.roll(jnp.where(first, odd, even), HD, 1)
        out_ref[:, columns] = (numer / total).astype(jnp.bfloat16)

    for pair in range(pairs):
        if pair == pairs // 2:
            take_summaries()
            for far in range(pairs):
                far_pair(far)
            for done in range(pair):
                finish_pair(done)
        near_pair(pair)
        if pair >= pairs // 2:
            finish_pair(pair)

    @pl.when(has_next)
    def _():
        for pair in range(pairs - ahead, pairs):
            near_wait_send(pair)

    for step in range(1, ctx_count):
        ctx_copy(step).wait_send()
    for step in range(1, grp_count):
        @pl.when(me_g + step < grp_count)
        def _():
            grp_copy(step).wait_send()


def shards(queries, keys, values, summary_pos):
    ctx_count = lax.axis_size("ctx")
    grp_count = lax.axis_size("grp")
    unused, tokens, width = queries.shape
    assert tokens == BLK and width == H * HD
    pairs = H // 2
    group_keys = ctx_count * SUMM
    all_keys = grp_count * group_keys
    vmem = pl.BlockSpec(memory_space=pltpu.VMEM)
    return pl.pallas_call(
        functools.partial(kernel, ctx_count, grp_count),
        out_shape=jax.ShapeDtypeStruct((tokens, width), jnp.bfloat16),
        in_specs=[pl.BlockSpec(memory_space=pl.ANY)] * 4,
        out_specs=vmem,
        scratch_shapes=[
            pltpu.VMEM((1, SUMM), jnp.int32),
            pltpu.VMEM((tokens, width), jnp.bfloat16),
            pltpu.VMEM((tokens, width), jnp.bfloat16),
            pltpu.VMEM((tokens, width), jnp.bfloat16),
            pltpu.VMEM((tokens, width), jnp.bfloat16),
            pltpu.VMEM((tokens, width), jnp.bfloat16),
            pltpu.VMEM((2 * SUMM, width), jnp.bfloat16),
            pltpu.VMEM((grp_count, ctx_count, 2 * SUMM, width), jnp.bfloat16),
            pltpu.VMEM((all_keys, width), jnp.bfloat16),
            pltpu.VMEM((all_keys, width), jnp.bfloat16),
            pltpu.VMEM((H, tokens, PAIR), jnp.float32),
            pltpu.VMEM((H, tokens, PAIR), jnp.float32),
            pltpu.SemaphoreType.DMA((2 * pairs,)),
            pltpu.SemaphoreType.DMA((2 * pairs,)),
            pltpu.SemaphoreType.DMA((ctx_count,)),
            pltpu.SemaphoreType.DMA((ctx_count,)),
            pltpu.SemaphoreType.DMA((grp_count,)),
            pltpu.SemaphoreType.DMA((grp_count,)),
            pltpu.SemaphoreType.DMA,
            pltpu.SemaphoreType.DMA((4,)),
        ],
        compiler_params=pltpu.CompilerParams(
            collective_id=0, has_side_effects=True, vmem_limit_bytes=56 * 1024 * 1024
        ),
    )(summary_pos[0], queries[0], keys[0], values[0])[None]


def solution(mesh):
    placed = (
        P("grp", "ctx", None),
        P("grp", "ctx", None),
        P("grp", "ctx", None),
        P("grp", "ctx", None),
    )
    return jax.shard_map(
        shards, mesh=mesh, in_specs=placed, out_specs=P("grp", "ctx", None), check_vma=False
    )
```

```python
import functools
import math

import jax
import jax.numpy as jnp
from jax import lax
from jax.experimental import pallas as pl
from jax.experimental.pallas import tpu as pltpu
from jax.sharding import PartitionSpec as P

H = 8
HD = 64
BLK = 512
SUMM = 8
PAIR = 2 * HD
SCALE_LOG2E = math.log2(math.e) / math.sqrt(HD)

masked_score = -1e30
MESH = pl.DeviceIdType.MESH


def at(grp, ctx):
    return (ctx, grp)


def scores_of(q, k):
    return lax.dot_general(q, k, (((1,), (1,)), ((), ())), preferred_element_type=jnp.float32)


def kernel(
    ctx_count, grp_count, pos_in, q_in, k_in, v_in, out_ref,
    pos_ref, q_ref, k_ref, v_ref, prev_k, prev_v, picked, gathered, sum_k, sum_v, peak_ref, acc_ref,
    near_send, near_recv, ctx_send, ctx_recv, grp_send, grp_recv, own_sem, load_sem,
):
    me_c = lax.axis_index("ctx")
    me_g = lax.axis_index("grp")
    flat = me_g * ctx_count + me_c
    pairs = H // 2
    early = 1
    ahead = pairs - 1
    half = BLK // 2
    rows_group = ctx_count * 2 * SUMM
    keys_group = ctx_count * SUMM
    at_last = me_c == ctx_count - 1
    has_next = flat < ctx_count * grp_count - 1
    has_prev = flat > 0

    def ctx_peer(step):
        return lax.rem(me_c + step, ctx_count)

    loads = [
        pltpu.make_async_copy(source, landing, load_sem.at[number])
        for number, (source, landing) in enumerate(
            ((pos_in, pos_ref), (k_in, k_ref), (v_in, v_ref), (q_in, q_ref))
        )
    ]
    for load in loads:
        load.start()

    barrier = pltpu.get_barrier_semaphore()
    for step in range(1, ctx_count):
        pl.semaphore_signal(barrier, inc=1, device_id=at(me_g, ctx_peer(step)), device_id_type=MESH)
    for step in range(1, grp_count):
        @pl.when(me_g >= step)
        def _():
            pl.semaphore_signal(barrier, inc=1, device_id=at(lax.rem(me_g - step + grp_count, grp_count), me_c), device_id_type=MESH)

    @pl.when((me_c == 0) & (me_g > 0))
    def _():
        pl.semaphore_signal(
            barrier, inc=1, device_id=at(lax.rem(me_g - 1 + grp_count, grp_count), ctx_count - 1), device_id_type=MESH
        )

    wraps = jnp.where(at_last & has_next, 1, 0)
    pl.semaphore_wait(barrier, ctx_count - 1 + grp_count - 1 - me_g + wraps)

    def ctx_copy(step):
        return pltpu.make_async_remote_copy(
            src_ref=picked,
            dst_ref=gathered.at[me_g, me_c],
            send_sem=ctx_send.at[step],
            recv_sem=ctx_recv.at[step],
            device_id=at(me_g, ctx_peer(step)),
            device_id_type=MESH,
        )

    def grp_copy(step):
        return pltpu.make_async_remote_copy(
            src_ref=gathered.at[me_g],
            dst_ref=gathered.at[me_g],
            send_sem=grp_send.at[step],
            recv_sem=grp_recv.at[step],
            device_id=at(lax.rem(me_g + step, grp_count), me_c),
            device_id_type=MESH,
        )

    def near_copy(pair, which):
        columns = pl.ds(pair * PAIR, PAIR)
        source, landing = ((k_in, prev_k), (v_in, prev_v))[which]
        wrap = lax.div(me_c + 1, ctx_count)
        return pltpu.make_async_remote_copy(
            src_ref=source.at[:, columns],
            dst_ref=landing.at[:, columns],
            send_sem=near_send.at[2 * pair + which],
            recv_sem=near_recv.at[2 * pair + which],
            device_id=at(lax.rem(me_g + wrap, grp_count), ctx_peer(1)),
            device_id_type=MESH,
        )

    def near_start(pair):
        near_copy(pair, 0).start()
        near_copy(pair, 1).start()

    def near_wait_send(pair):
        near_copy(pair, 0).wait_send()
        near_copy(pair, 1).wait_send()

    @pl.when(has_next)
    def _():
        near_start(0)

    for load in loads[:3]:
        load.wait()
    row = lax.broadcasted_iota(jnp.int32, (2 * SUMM, SUMM), 0)
    slot = lax.broadcasted_iota(jnp.int32, (2 * SUMM, SUMM), 1)
    position = pos_ref[...].astype(jnp.float32)
    target = jnp.where((row & (SUMM - 1)) == slot, position, 0.0).sum(-1, keepdims=True)
    column = lax.broadcasted_iota(jnp.int32, (2 * SUMM, BLK), 1)
    choose = jnp.where(column == target.astype(jnp.int32), 1.0, 0.0).astype(jnp.bfloat16)
    chosen_k = jnp.dot(choose, k_ref[...], preferred_element_type=jnp.float32)
    chosen_v = jnp.dot(choose, v_ref[...], preferred_element_type=jnp.float32)
    wide_row = lax.broadcasted_iota(jnp.int32, chosen_k.shape, 0)
    picked[...] = jnp.where(wide_row < SUMM, chosen_k, chosen_v).astype(jnp.bfloat16)

    for step in range(1, ctx_count):
        ctx_copy(step).start()

    @pl.when(has_next)
    def _():
        for pair in range(1, ahead):
            near_start(pair)

    own_copy = pltpu.make_async_copy(
        picked,
        gathered.at[me_g, me_c],
        own_sem,
    )
    own_copy.start()
    loads[3].wait()

    lane = lax.broadcasted_iota(jnp.int32, (1, PAIR), 1)
    in_head = [
        jnp.where((lane < HD) == (side == 0), 1.0, 0.0).astype(jnp.bfloat16) for side in range(2)
    ]
    off_head = [in_head[1], in_head[0]]

    def weighed(scores, peak, vals, side):
        weights = jnp.exp2((scores - peak) * SCALE_LOG2E).astype(jnp.bfloat16)
        vals_ones = vals * in_head[side] + off_head[side]
        return jnp.dot(weights, vals_ones, preferred_element_type=jnp.float32)

    def fold(head, side, q, keys, vals, allowed):
        scores = scores_of(q * in_head[side], keys)
        if allowed is not None:
            scores = jnp.where(allowed, scores, masked_score)
        old = peak_ref[head][:, :1]
        peak = jnp.maximum(old, scores.max(-1, keepdims=True))
        part = weighed(scores, peak, vals, side)
        rescale = jnp.exp2((old - peak) * SCALE_LOG2E)
        peak_ref[head] = jnp.broadcast_to(peak, (BLK, PAIR))
        return acc_ref[head] * rescale + part

    def columns_of(pair):
        return pl.ds(pair * PAIR, PAIR)

    def own_pair(pair):
        columns = columns_of(pair)
        for side in range(2):
            head = 2 * pair + side
            for part in range(2):
                rows = pl.ds(part * half, half)
                count = (part + 1) * half
                q = q_ref[rows, columns] * in_head[side]
                scores = scores_of(q, k_ref[pl.ds(0, count), columns])
                u = lax.broadcasted_iota(jnp.int32, scores.shape, 1)
                t = lax.broadcasted_iota(jnp.int32, scores.shape, 0) + part * half
                scores = jnp.where(u <= t, scores, masked_score)
                peak = scores.max(-1, keepdims=True)
                acc_ref[head, rows] = weighed(scores, peak, v_ref[pl.ds(0, count), columns], side)
                peak_ref[head, rows] = jnp.broadcast_to(peak, (half, PAIR))

    for pair in range(early):
        own_pair(pair)

    own_copy.wait()
    for step in range(1, ctx_count):
        ctx_copy(step).wait_recv()

    for step in range(1, grp_count):
        @pl.when(me_g + step < grp_count)
        def _():
            grp_copy(step).start()

    for pair in range(early, pairs):
        own_pair(pair)

    key_row = lax.broadcasted_iota(jnp.int32, (keys_group, rows_group), 0)
    source_row = lax.broadcasted_iota(jnp.int32, (keys_group, rows_group), 1)
    wanted = key_row * 2 - (key_row & (SUMM - 1))
    take_k = jnp.where(source_row == wanted, 1.0, 0.0).astype(jnp.bfloat16)
    take_v = jnp.where(source_row == wanted + SUMM, 1.0, 0.0).astype(jnp.bfloat16)
    def take_summaries():
        for step in range(1, grp_count):
            @pl.when(me_g >= step)
            def _():
                grp_copy(step).wait_recv()

        for group in range(grp_count):
            rows = pl.ds(group * keys_group, keys_group)

            @pl.when(me_g >= group)
            def _():
                block = gathered[group].reshape(rows_group, k_ref.shape[1])
                sum_k[rows] = jnp.dot(take_k, block, preferred_element_type=jnp.float32).astype(
                    jnp.bfloat16
                )
                sum_v[rows] = jnp.dot(take_v, block, preferred_element_type=jnp.float32).astype(
                    jnp.bfloat16
                )

            @pl.when(me_g < group)
            def _():
                sum_k[rows] = jnp.zeros((keys_group, k_ref.shape[1]), jnp.bfloat16)
                sum_v[rows] = jnp.zeros((keys_group, k_ref.shape[1]), jnp.bfloat16)

    summ_rows = grp_count * keys_group
    tile = math.gcd(summ_rows, BLK)

    def far_pair(pair):
        columns = columns_of(pair)

        def far_tile(index, inner):
            rows = pl.ds(index * tile, tile)
            key_index = lax.broadcasted_iota(jnp.int32, (1, tile), 1) + index * tile
            allowed = key_index < (flat - 1) * SUMM
            for side in range(2):
                head = 2 * pair + side
                acc_ref[head] = fold(
                    head, side, q_ref[:, columns], sum_k[rows, columns], sum_v[rows, columns],
                    allowed,
                )
            return inner

        if summ_rows == tile:
            return far_tile(0, None)
        return lax.fori_loop(0, summ_rows // tile, far_tile, None)

    def near_pair(pair):
        columns = columns_of(pair)

        if pair + ahead < pairs:
            @pl.when(has_next)
            def _():
                near_wait_send(pair)
                near_start(pair + ahead)

        @pl.when(has_prev)
        def _():
            near_copy(pair, 0).wait_recv()
            near_copy(pair, 1).wait_recv()
            for side in range(2):
                head = 2 * pair + side
                acc_ref[head] = fold(
                    head, side, q_ref[:, columns], prev_k[:, columns], prev_v[:, columns], None
                )

    def finish_pair(pair):
        columns = columns_of(pair)
        even, odd = acc_ref[2 * pair], acc_ref[2 * pair + 1]
        first = lane < HD
        numer = jnp.where(first, even, odd)
        total = pltpu.roll(jnp.where(first, odd, even), HD, 1)
        out_ref[:, columns] = (numer / total).astype(jnp.bfloat16)

    for pair in range(pairs):
        if pair == pairs // 2:
            take_summaries()
            for far in range(pairs):
                far_pair(far)
            for done in range(pair):
                finish_pair(done)
        near_pair(pair)
        if pair >= pairs // 2:
            finish_pair(pair)

    @pl.when(has_next)
    def _():
        for pair in range(pairs - ahead, pairs):
            near_wait_send(pair)

    for step in range(1, ctx_count):
        ctx_copy(step).wait_send()
    for step in range(1, grp_count):
        @pl.when(me_g + step < grp_count)
        def _():
            grp_copy(step).wait_send()


def shards(queries, keys, values, summary_pos):
    ctx_count = lax.axis_size("ctx")
    grp_count = lax.axis_size("grp")
    unused, tokens, width = queries.shape
    assert tokens == BLK and width == H * HD
    pairs = H // 2
    group_keys = ctx_count * SUMM
    all_keys = grp_count * group_keys
    vmem = pl.BlockSpec(memory_space=pltpu.VMEM)
    return pl.pallas_call(
        functools.partial(kernel, ctx_count, grp_count),
        out_shape=jax.ShapeDtypeStruct((tokens, width), jnp.bfloat16),
        in_specs=[pl.BlockSpec(memory_space=pl.ANY)] * 4,
        out_specs=vmem,
        scratch_shapes=[
            pltpu.VMEM((1, SUMM), jnp.int32),
            pltpu.VMEM((tokens, width), jnp.bfloat16),
            pltpu.VMEM((tokens, width), jnp.bfloat16),
            pltpu.VMEM((tokens, width), jnp.bfloat16),
            pltpu.VMEM((tokens, width), jnp.bfloat16),
            pltpu.VMEM((tokens, width), jnp.bfloat16),
            pltpu.VMEM((2 * SUMM, width), jnp.bfloat16),
            pltpu.VMEM((grp_count, ctx_count, 2 * SUMM, width), jnp.bfloat16),
            pltpu.VMEM((all_keys, width), jnp.bfloat16),
            pltpu.VMEM((all_keys, width), jnp.bfloat16),
            pltpu.VMEM((H, tokens, PAIR), jnp.float32),
            pltpu.VMEM((H, tokens, PAIR), jnp.float32),
            pltpu.SemaphoreType.DMA((2 * pairs,)),
            pltpu.SemaphoreType.DMA((2 * pairs,)),
            pltpu.SemaphoreType.DMA((ctx_count,)),
            pltpu.SemaphoreType.DMA((ctx_count,)),
            pltpu.SemaphoreType.DMA((grp_count,)),
            pltpu.SemaphoreType.DMA((grp_count,)),
            pltpu.SemaphoreType.DMA,
            pltpu.SemaphoreType.DMA((4,)),
        ],
        compiler_params=pltpu.CompilerParams(
            collective_id=0, has_side_effects=True, vmem_limit_bytes=56 * 1024 * 1024
        ),
    )(summary_pos[0], queries[0], keys[0], values[0])[None]


def solution(mesh):
    placed = (
        P("grp", "ctx", None),
        P("grp", "ctx", None),
        P("grp", "ctx", None),
        P("grp", "ctx", None),
    )
    return jax.shard_map(
        shards, mesh=mesh, in_specs=placed, out_specs=P("grp", "ctx", None), check_vma=False
    )
```

```python
import functools
import math

import jax
import jax.numpy as jnp
from jax import lax
from jax.experimental import pallas as pl
from jax.experimental.pallas import tpu as pltpu
from jax.sharding import PartitionSpec as P

H = 8
HD = 64
BLK = 512
SUMM = 8
PAIR = 2 * HD
SCALE_LOG2E = math.log2(math.e) / math.sqrt(HD)

masked_score = -1e30
MESH = pl.DeviceIdType.MESH


def at(grp, ctx):
    return (ctx, grp)


def scores_of(q, k):
    return lax.dot_general(q, k, (((1,), (1,)), ((), ())), preferred_element_type=jnp.float32)


def kernel(
    ctx_count, grp_count, pos_in, q_in, k_in, v_in, out_ref,
    pos_ref, q_ref, k_ref, v_ref, prev_k, prev_v, picked, gathered, sum_k, sum_v, peak_ref, acc_ref,
    near_send, near_recv, ctx_send, ctx_recv, grp_send, grp_recv, own_sem, load_sem,
    relay, relay_send, relay_recv, onward_send,
):
    me_c = lax.axis_index("ctx")
    me_g = lax.axis_index("grp")
    flat = me_g * ctx_count + me_c
    pairs = H // 2
    early = 1
    relayed = pairs // 2
    first_ctx = me_c == 0
    relays = first_ctx & (me_g < grp_count - 1)
    half = BLK // 2
    rows_group = ctx_count * 2 * SUMM
    keys_group = ctx_count * SUMM
    at_last = me_c == ctx_count - 1
    has_next = flat < ctx_count * grp_count - 1
    has_prev = flat > 0

    def ctx_peer(step):
        return lax.rem(me_c + step, ctx_count)

    loads = [
        pltpu.make_async_copy(source, landing, load_sem.at[number])
        for number, (source, landing) in enumerate(
            ((pos_in, pos_ref), (k_in, k_ref), (v_in, v_ref), (q_in, q_ref))
        )
    ]
    for load in loads:
        load.start()

    barrier = pltpu.get_barrier_semaphore()
    for step in range(1, ctx_count):
        pl.semaphore_signal(barrier, inc=1, device_id=at(me_g, ctx_peer(step)), device_id_type=MESH)
    for step in range(1, grp_count):
        @pl.when(me_g >= step)
        def _():
            pl.semaphore_signal(barrier, inc=1, device_id=at(lax.rem(me_g - step + grp_count, grp_count), me_c), device_id_type=MESH)

    @pl.when((me_c == 0) & (me_g > 0))
    def _():
        pl.semaphore_signal(
            barrier, inc=1, device_id=at(lax.rem(me_g - 1 + grp_count, grp_count), ctx_count - 1), device_id_type=MESH
        )

    wraps = jnp.where(at_last & has_next, 1, 0)
    pl.semaphore_wait(barrier, ctx_count - 1 + grp_count - 1 - me_g + wraps)

    def ctx_copy(step):
        return pltpu.make_async_remote_copy(
            src_ref=picked,
            dst_ref=gathered.at[me_g, me_c],
            send_sem=ctx_send.at[step],
            recv_sem=ctx_recv.at[step],
            device_id=at(me_g, ctx_peer(step)),
            device_id_type=MESH,
        )

    def grp_copy(step):
        return pltpu.make_async_remote_copy(
            src_ref=gathered.at[me_g],
            dst_ref=gathered.at[me_g],
            send_sem=grp_send.at[step],
            recv_sem=grp_recv.at[step],
            device_id=at(lax.rem(me_g + step, grp_count), me_c),
            device_id_type=MESH,
        )

    def near_copy(pair, which):
        columns = pl.ds(pair * PAIR, PAIR)
        source, landing = ((k_in, prev_k), (v_in, prev_v))[which]
        wrap = lax.div(me_c + 1, ctx_count)
        return pltpu.make_async_remote_copy(
            src_ref=source.at[:, columns],
            dst_ref=landing.at[:, columns],
            send_sem=near_send.at[2 * pair + which],
            recv_sem=near_recv.at[2 * pair + which],
            device_id=at(lax.rem(me_g + wrap, grp_count), ctx_peer(1)),
            device_id_type=MESH,
        )

    def relay_copy(pair, which):
        slot = 2 * (pair - relayed) + which
        return pltpu.make_async_remote_copy(
            src_ref=(k_in, v_in)[which].at[:, pl.ds(pair * PAIR, PAIR)],
            dst_ref=relay.at[slot],
            send_sem=relay_send.at[slot],
            recv_sem=relay_recv.at[slot],
            device_id=at(me_g, ctx_peer(1)),
            device_id_type=MESH,
        )

    def onward_copy(pair, which):
        slot = 2 * (pair - relayed) + which
        return pltpu.make_async_remote_copy(
            src_ref=relay.at[slot],
            dst_ref=(prev_k, prev_v)[which].at[:, pl.ds(pair * PAIR, PAIR)],
            send_sem=onward_send.at[slot],
            recv_sem=near_recv.at[2 * pair + which],
            device_id=at(lax.rem(me_g + 1, grp_count), me_c),
            device_id_type=MESH,
        )

    def near_each(pair, act):
        if pair < relayed:
            for which in range(2):
                act(near_copy(pair, which))
            return

        @pl.when(at_last)
        def _():
            for which in range(2):
                act(relay_copy(pair, which))

        @pl.when(~at_last)
        def _():
            for which in range(2):
                act(near_copy(pair, which))

    def near_start(pair):
        near_each(pair, lambda copy: copy.start())

    def near_wait_send(pair):
        near_each(pair, lambda copy: copy.wait_send())

    @pl.when(has_next)
    def _():
        near_start(0)

    for load in loads[:3]:
        load.wait()
    row = lax.broadcasted_iota(jnp.int32, (2 * SUMM, SUMM), 0)
    slot = lax.broadcasted_iota(jnp.int32, (2 * SUMM, SUMM), 1)
    position = pos_ref[...].astype(jnp.float32)
    target = jnp.where((row & (SUMM - 1)) == slot, position, 0.0).sum(-1, keepdims=True)
    column = lax.broadcasted_iota(jnp.int32, (2 * SUMM, BLK), 1)
    choose = jnp.where(column == target.astype(jnp.int32), 1.0, 0.0).astype(jnp.bfloat16)
    chosen_k = jnp.dot(choose, k_ref[...], preferred_element_type=jnp.float32)
    chosen_v = jnp.dot(choose, v_ref[...], preferred_element_type=jnp.float32)
    wide_row = lax.broadcasted_iota(jnp.int32, chosen_k.shape, 0)
    picked[...] = jnp.where(wide_row < SUMM, chosen_k, chosen_v).astype(jnp.bfloat16)

    for step in range(1, ctx_count):
        ctx_copy(step).start()

    @pl.when(has_next)
    def _():
        for pair in range(1, pairs):
            near_start(pair)

    own_copy = pltpu.make_async_copy(
        picked,
        gathered.at[me_g, me_c],
        own_sem,
    )
    own_copy.start()
    loads[3].wait()

    lane = lax.broadcasted_iota(jnp.int32, (1, PAIR), 1)
    in_head = [
        jnp.where((lane < HD) == (side == 0), 1.0, 0.0).astype(jnp.bfloat16) for side in range(2)
    ]
    off_head = [in_head[1], in_head[0]]

    def weighed(scores, peak, vals, side):
        weights = jnp.exp2((scores - peak) * SCALE_LOG2E).astype(jnp.bfloat16)
        vals_ones = vals * in_head[side] + off_head[side]
        return jnp.dot(weights, vals_ones, preferred_element_type=jnp.float32)

    def fold(head, side, q, keys, vals, allowed):
        scores = scores_of(q * in_head[side], keys)
        if allowed is not None:
            scores = jnp.where(allowed, scores, masked_score)
        old = peak_ref[head][:, :1]
        peak = jnp.maximum(old, scores.max(-1, keepdims=True))
        part = weighed(scores, peak, vals, side)
        rescale = jnp.exp2((old - peak) * SCALE_LOG2E)
        peak_ref[head] = jnp.broadcast_to(peak, (BLK, PAIR))
        return acc_ref[head] * rescale + part

    def columns_of(pair):
        return pl.ds(pair * PAIR, PAIR)

    def own_pair(pair):
        columns = columns_of(pair)
        for side in range(2):
            head = 2 * pair + side
            for part in range(2):
                rows = pl.ds(part * half, half)
                count = (part + 1) * half
                q = q_ref[rows, columns] * in_head[side]
                scores = scores_of(q, k_ref[pl.ds(0, count), columns])
                u = lax.broadcasted_iota(jnp.int32, scores.shape, 1)
                t = lax.broadcasted_iota(jnp.int32, scores.shape, 0) + part * half
                scores = jnp.where(u <= t, scores, masked_score)
                peak = scores.max(-1, keepdims=True)
                acc_ref[head, rows] = weighed(scores, peak, v_ref[pl.ds(0, count), columns], side)
                peak_ref[head, rows] = jnp.broadcast_to(peak, (half, PAIR))

    for pair in range(early):
        own_pair(pair)

    own_copy.wait()
    for step in range(1, ctx_count):
        ctx_copy(step).wait_recv()

    for step in range(1, grp_count):
        @pl.when(me_g + step < grp_count)
        def _():
            grp_copy(step).start()

    for pair in range(early, pairs):
        own_pair(pair)

    key_row = lax.broadcasted_iota(jnp.int32, (keys_group, rows_group), 0)
    source_row = lax.broadcasted_iota(jnp.int32, (keys_group, rows_group), 1)
    wanted = key_row * 2 - (key_row & (SUMM - 1))
    take_k = jnp.where(source_row == wanted, 1.0, 0.0).astype(jnp.bfloat16)
    take_v = jnp.where(source_row == wanted + SUMM, 1.0, 0.0).astype(jnp.bfloat16)
    def take_summaries():
        for step in range(1, grp_count):
            @pl.when(me_g >= step)
            def _():
                grp_copy(step).wait_recv()

        for group in range(grp_count):
            rows = pl.ds(group * keys_group, keys_group)

            @pl.when(me_g >= group)
            def _():
                block = gathered[group].reshape(rows_group, k_ref.shape[1])
                sum_k[rows] = jnp.dot(take_k, block, preferred_element_type=jnp.float32).astype(
                    jnp.bfloat16
                )
                sum_v[rows] = jnp.dot(take_v, block, preferred_element_type=jnp.float32).astype(
                    jnp.bfloat16
                )

            @pl.when(me_g < group)
            def _():
                sum_k[rows] = jnp.zeros((keys_group, k_ref.shape[1]), jnp.bfloat16)
                sum_v[rows] = jnp.zeros((keys_group, k_ref.shape[1]), jnp.bfloat16)

    summ_rows = grp_count * keys_group
    tile = math.gcd(summ_rows, BLK)

    def far_pair(pair):
        columns = columns_of(pair)

        def far_tile(index, inner):
            rows = pl.ds(index * tile, tile)
            key_index = lax.broadcasted_iota(jnp.int32, (1, tile), 1) + index * tile
            allowed = key_index < (flat - 1) * SUMM
            for side in range(2):
                head = 2 * pair + side
                acc_ref[head] = fold(
                    head, side, q_ref[:, columns], sum_k[rows, columns], sum_v[rows, columns],
                    allowed,
                )
            return inner

        if summ_rows == tile:
            return far_tile(0, None)
        return lax.fori_loop(0, summ_rows // tile, far_tile, None)

    def near_pair(pair):
        columns = columns_of(pair)

        @pl.when(has_prev)
        def _():
            near_copy(pair, 0).wait_recv()
            near_copy(pair, 1).wait_recv()
            for side in range(2):
                head = 2 * pair + side
                acc_ref[head] = fold(
                    head, side, q_ref[:, columns], prev_k[:, columns], prev_v[:, columns], None
                )

    def finish_pair(pair):
        columns = columns_of(pair)
        even, odd = acc_ref[2 * pair], acc_ref[2 * pair + 1]
        first = lane < HD
        numer = jnp.where(first, even, odd)
        total = pltpu.roll(jnp.where(first, odd, even), HD, 1)
        out_ref[:, columns] = (numer / total).astype(jnp.bfloat16)

    @pl.when(relays)
    def _():
        for pair in range(relayed, pairs):
            for which in range(2):
                relay_copy(pair, which).wait_recv()
                onward_copy(pair, which).start()

    for pair in range(pairs):
        if pair == pairs // 2:
            take_summaries()
            for far in range(pairs):
                far_pair(far)
            for done in range(pair):
                finish_pair(done)
        near_pair(pair)
        if pair >= pairs // 2:
            finish_pair(pair)

    @pl.when(has_next)
    def _():
        for pair in range(pairs):
            near_wait_send(pair)

    @pl.when(relays)
    def _():
        for pair in range(relayed, pairs):
            for which in range(2):
                onward_copy(pair, which).wait_send()

    for step in range(1, ctx_count):
        ctx_copy(step).wait_send()
    for step in range(1, grp_count):
        @pl.when(me_g + step < grp_count)
        def _():
            grp_copy(step).wait_send()


def shards(queries, keys, values, summary_pos):
    ctx_count = lax.axis_size("ctx")
    grp_count = lax.axis_size("grp")
    unused, tokens, width = queries.shape
    assert tokens == BLK and width == H * HD
    pairs = H // 2
    group_keys = ctx_count * SUMM
    all_keys = grp_count * group_keys
    vmem = pl.BlockSpec(memory_space=pltpu.VMEM)
    return pl.pallas_call(
        functools.partial(kernel, ctx_count, grp_count),
        out_shape=jax.ShapeDtypeStruct((tokens, width), jnp.bfloat16),
        in_specs=[pl.BlockSpec(memory_space=pl.ANY)] * 4,
        out_specs=vmem,
        scratch_shapes=[
            pltpu.VMEM((1, SUMM), jnp.int32),
            pltpu.VMEM((tokens, width), jnp.bfloat16),
            pltpu.VMEM((tokens, width), jnp.bfloat16),
            pltpu.VMEM((tokens, width), jnp.bfloat16),
            pltpu.VMEM((tokens, width), jnp.bfloat16),
            pltpu.VMEM((tokens, width), jnp.bfloat16),
            pltpu.VMEM((2 * SUMM, width), jnp.bfloat16),
            pltpu.VMEM((grp_count, ctx_count, 2 * SUMM, width), jnp.bfloat16),
            pltpu.VMEM((all_keys, width), jnp.bfloat16),
            pltpu.VMEM((all_keys, width), jnp.bfloat16),
            pltpu.VMEM((H, tokens, PAIR), jnp.float32),
            pltpu.VMEM((H, tokens, PAIR), jnp.float32),
            pltpu.SemaphoreType.DMA((2 * pairs,)),
            pltpu.SemaphoreType.DMA((2 * pairs,)),
            pltpu.SemaphoreType.DMA((ctx_count,)),
            pltpu.SemaphoreType.DMA((ctx_count,)),
            pltpu.SemaphoreType.DMA((grp_count,)),
            pltpu.SemaphoreType.DMA((grp_count,)),
            pltpu.SemaphoreType.DMA,
            pltpu.SemaphoreType.DMA((4,)),
            pltpu.VMEM((pairs, tokens, PAIR), jnp.bfloat16),
            pltpu.SemaphoreType.DMA((pairs,)),
            pltpu.SemaphoreType.DMA((pairs,)),
            pltpu.SemaphoreType.DMA((pairs,)),
        ],
        compiler_params=pltpu.CompilerParams(
            collective_id=0, has_side_effects=True, vmem_limit_bytes=56 * 1024 * 1024
        ),
    )(summary_pos[0], queries[0], keys[0], values[0])[None]


def solution(mesh):
    placed = (
        P("grp", "ctx", None),
        P("grp", "ctx", None),
        P("grp", "ctx", None),
        P("grp", "ctx", None),
    )
    return jax.shard_map(
        shards, mesh=mesh, in_specs=placed, out_specs=P("grp", "ctx", None), check_vma=False
    )
```

```python
import functools
import math

import jax
import jax.numpy as jnp
from jax import lax
from jax.experimental import pallas as pl
from jax.experimental.pallas import tpu as pltpu
from jax.sharding import PartitionSpec as P

H = 8
HD = 64
BLK = 512
SUMM = 8
PAIR = 2 * HD
SCALE_LOG2E = math.log2(math.e) / math.sqrt(HD)

masked_score = -1e30
MESH = pl.DeviceIdType.MESH


def at(grp, ctx):
    return (ctx, grp)


def scores_of(q, k):
    return lax.dot_general(q, k, (((1,), (1,)), ((), ())), preferred_element_type=jnp.float32)


def kernel(
    ctx_count, grp_count, pos_in, q_in, k_in, v_in, out_ref,
    pos_ref, q_ref, k_ref, v_ref, prev_k, prev_v, picked, gathered, sum_k, sum_v, peak_ref, acc_ref,
    near_send, near_recv, ctx_send, ctx_recv, grp_send, grp_recv, own_sem, load_sem,
):
    me_c = lax.axis_index("ctx")
    me_g = lax.axis_index("grp")
    flat = me_g * ctx_count + me_c
    pairs = H // 2
    early = 1
    ahead = pairs
    half = BLK // 2
    rows_group = ctx_count * 2 * SUMM
    keys_group = ctx_count * SUMM
    at_last = me_c == ctx_count - 1
    has_next = flat < ctx_count * grp_count - 1
    has_prev = flat > 0

    def ctx_peer(step):
        return lax.rem(me_c + step, ctx_count)

    loads = [
        pltpu.make_async_copy(source, landing, load_sem.at[number])
        for number, (source, landing) in enumerate(
            ((pos_in, pos_ref), (k_in, k_ref), (v_in, v_ref), (q_in, q_ref))
        )
    ]
    for load in loads:
        load.start()

    barrier = pltpu.get_barrier_semaphore()
    for step in range(1, ctx_count):
        pl.semaphore_signal(barrier, inc=1, device_id=at(me_g, ctx_peer(step)), device_id_type=MESH)
    for step in range(1, grp_count):
        @pl.when(me_g >= step)
        def _():
            pl.semaphore_signal(barrier, inc=1, device_id=at(lax.rem(me_g - step + grp_count, grp_count), me_c), device_id_type=MESH)

    @pl.when((me_c == 0) & (me_g > 0))
    def _():
        pl.semaphore_signal(
            barrier, inc=1, device_id=at(lax.rem(me_g - 1 + grp_count, grp_count), ctx_count - 1), device_id_type=MESH
        )

    wraps = jnp.where(at_last & has_next, 1, 0)
    pl.semaphore_wait(barrier, ctx_count - 1 + grp_count - 1 - me_g + wraps)

    def ctx_copy(step):
        return pltpu.make_async_remote_copy(
            src_ref=picked,
            dst_ref=gathered.at[me_g, me_c],
            send_sem=ctx_send.at[step],
            recv_sem=ctx_recv.at[step],
            device_id=at(me_g, ctx_peer(step)),
            device_id_type=MESH,
        )

    def grp_copy(step):
        return pltpu.make_async_remote_copy(
            src_ref=gathered.at[me_g],
            dst_ref=gathered.at[me_g],
            send_sem=grp_send.at[step],
            recv_sem=grp_recv.at[step],
            device_id=at(lax.rem(me_g + step, grp_count), me_c),
            device_id_type=MESH,
        )

    def near_copy(pair, which):
        columns = pl.ds(pair * PAIR, PAIR)
        source, landing = ((k_in, prev_k), (v_in, prev_v))[which]
        wrap = lax.div(me_c + 1, ctx_count)
        return pltpu.make_async_remote_copy(
            src_ref=source.at[:, columns],
            dst_ref=landing.at[:, columns],
            send_sem=near_send.at[2 * pair + which],
            recv_sem=near_recv.at[2 * pair + which],
            device_id=at(lax.rem(me_g + wrap, grp_count), ctx_peer(1)),
            device_id_type=MESH,
        )

    def near_start(pair):
        near_copy(pair, 0).start()
        near_copy(pair, 1).start()

    def near_wait_send(pair):
        near_copy(pair, 0).wait_send()
        near_copy(pair, 1).wait_send()

    @pl.when(has_next)
    def _():
        near_start(0)

    for load in loads[:3]:
        load.wait()
    row = lax.broadcasted_iota(jnp.int32, (2 * SUMM, SUMM), 0)
    slot = lax.broadcasted_iota(jnp.int32, (2 * SUMM, SUMM), 1)
    position = pos_ref[...].astype(jnp.float32)
    target = jnp.where((row & (SUMM - 1)) == slot, position, 0.0).sum(-1, keepdims=True)
    column = lax.broadcasted_iota(jnp.int32, (2 * SUMM, BLK), 1)
    choose = jnp.where(column == target.astype(jnp.int32), 1.0, 0.0).astype(jnp.bfloat16)
    chosen_k = jnp.dot(choose, k_ref[...], preferred_element_type=jnp.float32)
    chosen_v = jnp.dot(choose, v_ref[...], preferred_element_type=jnp.float32)
    wide_row = lax.broadcasted_iota(jnp.int32, chosen_k.shape, 0)
    picked[...] = jnp.where(wide_row < SUMM, chosen_k, chosen_v).astype(jnp.bfloat16)

    for step in range(1, ctx_count):
        ctx_copy(step).start()

    @pl.when(has_next)
    def _():
        for pair in range(1, ahead):
            near_start(pair)

    own_copy = pltpu.make_async_copy(
        picked,
        gathered.at[me_g, me_c],
        own_sem,
    )
    own_copy.start()
    loads[3].wait()

    lane = lax.broadcasted_iota(jnp.int32, (1, PAIR), 1)
    in_head = [
        jnp.where((lane < HD) == (side == 0), 1.0, 0.0).astype(jnp.bfloat16) for side in range(2)
    ]
    off_head = [in_head[1], in_head[0]]

    def weighed(scores, peak, vals, side):
        weights = jnp.exp2((scores - peak) * SCALE_LOG2E).astype(jnp.bfloat16)
        vals_ones = vals * in_head[side] + off_head[side]
        return jnp.dot(weights, vals_ones, preferred_element_type=jnp.float32)

    def fold(head, side, q, keys, vals, allowed):
        scores = scores_of(q * in_head[side], keys)
        if allowed is not None:
            scores = jnp.where(allowed, scores, masked_score)
        old = peak_ref[head][:, :1]
        peak = jnp.maximum(old, scores.max(-1, keepdims=True))
        part = weighed(scores, peak, vals, side)
        rescale = jnp.exp2((old - peak) * SCALE_LOG2E)
        peak_ref[head] = jnp.broadcast_to(peak, (BLK, PAIR))
        return acc_ref[head] * rescale + part

    def columns_of(pair):
        return pl.ds(pair * PAIR, PAIR)

    def own_pair(pair):
        columns = columns_of(pair)
        for side in range(2):
            head = 2 * pair + side
            for part in range(2):
                rows = pl.ds(part * half, half)
                count = (part + 1) * half
                q = q_ref[rows, columns] * in_head[side]
                scores = scores_of(q, k_ref[pl.ds(0, count), columns])
                u = lax.broadcasted_iota(jnp.int32, scores.shape, 1)
                t = lax.broadcasted_iota(jnp.int32, scores.shape, 0) + part * half
                scores = jnp.where(u <= t, scores, masked_score)
                peak = scores.max(-1, keepdims=True)
                acc_ref[head, rows] = weighed(scores, peak, v_ref[pl.ds(0, count), columns], side)
                peak_ref[head, rows] = jnp.broadcast_to(peak, (half, PAIR))

    for pair in range(early):
        own_pair(pair)

    own_copy.wait()
    for step in range(1, ctx_count):
        ctx_copy(step).wait_recv()

    for step in range(1, grp_count):
        @pl.when(me_g + step < grp_count)
        def _():
            grp_copy(step).start()

    for pair in range(early, pairs):
        own_pair(pair)

    key_row = lax.broadcasted_iota(jnp.int32, (keys_group, rows_group), 0)
    source_row = lax.broadcasted_iota(jnp.int32, (keys_group, rows_group), 1)
    wanted = key_row * 2 - (key_row & (SUMM - 1))
    take_k = jnp.where(source_row == wanted, 1.0, 0.0).astype(jnp.bfloat16)
    take_v = jnp.where(source_row == wanted + SUMM, 1.0, 0.0).astype(jnp.bfloat16)
    def take_summaries():
        for step in range(1, grp_count):
            @pl.when(me_g >= step)
            def _():
                grp_copy(step).wait_recv()

        for group in range(grp_count):
            rows = pl.ds(group * keys_group, keys_group)

            @pl.when(me_g >= group)
            def _():
                block = gathered[group].reshape(rows_group, k_ref.shape[1])
                sum_k[rows] = jnp.dot(take_k, block, preferred_element_type=jnp.float32).astype(
                    jnp.bfloat16
                )
                sum_v[rows] = jnp.dot(take_v, block, preferred_element_type=jnp.float32).astype(
                    jnp.bfloat16
                )

            @pl.when(me_g < group)
            def _():
                sum_k[rows] = jnp.zeros((keys_group, k_ref.shape[1]), jnp.bfloat16)
                sum_v[rows] = jnp.zeros((keys_group, k_ref.shape[1]), jnp.bfloat16)

    summ_rows = grp_count * keys_group
    tile = math.gcd(summ_rows, BLK)

    def far_pair(pair):
        columns = columns_of(pair)

        def far_tile(index, inner):
            rows = pl.ds(index * tile, tile)
            key_index = lax.broadcasted_iota(jnp.int32, (1, tile), 1) + index * tile
            allowed = key_index < (flat - 1) * SUMM
            for side in range(2):
                head = 2 * pair + side
                acc_ref[head] = fold(
                    head, side, q_ref[:, columns], sum_k[rows, columns], sum_v[rows, columns],
                    allowed,
                )
            return inner

        if summ_rows == tile:
            return far_tile(0, None)
        return lax.fori_loop(0, summ_rows // tile, far_tile, None)

    def near_pair(pair):
        columns = columns_of(pair)

        if pair + ahead < pairs:
            @pl.when(has_next)
            def _():
                near_wait_send(pair)
                near_start(pair + ahead)

        @pl.when(has_prev)
        def _():
            near_copy(pair, 0).wait_recv()
            near_copy(pair, 1).wait_recv()
            for side in range(2):
                head = 2 * pair + side
                acc_ref[head] = fold(
                    head, side, q_ref[:, columns], prev_k[:, columns], prev_v[:, columns], None
                )

    def finish_pair(pair):
        columns = columns_of(pair)
        even, odd = acc_ref[2 * pair], acc_ref[2 * pair + 1]
        first = lane < HD
        numer = jnp.where(first, even, odd)
        total = pltpu.roll(jnp.where(first, odd, even), HD, 1)
        out_ref[:, columns] = (numer / total).astype(jnp.bfloat16)

    for pair in range(pairs):
        if pair == pairs // 2:
            take_summaries()
            for far in range(pairs):
                far_pair(far)
            for done in range(pair):
                finish_pair(done)
        near_pair(pair)
        if pair >= pairs // 2:
            finish_pair(pair)

    @pl.when(has_next)
    def _():
        for pair in range(pairs - ahead, pairs):
            near_wait_send(pair)

    for step in range(1, ctx_count):
        ctx_copy(step).wait_send()
    for step in range(1, grp_count):
        @pl.when(me_g + step < grp_count)
        def _():
            grp_copy(step).wait_send()


def shards(queries, keys, values, summary_pos):
    ctx_count = lax.axis_size("ctx")
    grp_count = lax.axis_size("grp")
    unused, tokens, width = queries.shape
    assert tokens == BLK and width == H * HD
    pairs = H // 2
    group_keys = ctx_count * SUMM
    all_keys = grp_count * group_keys
    vmem = pl.BlockSpec(memory_space=pltpu.VMEM)
    return pl.pallas_call(
        functools.partial(kernel, ctx_count, grp_count),
        out_shape=jax.ShapeDtypeStruct((tokens, width), jnp.bfloat16),
        in_specs=[pl.BlockSpec(memory_space=pl.ANY)] * 4,
        out_specs=vmem,
        scratch_shapes=[
            pltpu.VMEM((1, SUMM), jnp.int32),
            pltpu.VMEM((tokens, width), jnp.bfloat16),
            pltpu.VMEM((tokens, width), jnp.bfloat16),
            pltpu.VMEM((tokens, width), jnp.bfloat16),
            pltpu.VMEM((tokens, width), jnp.bfloat16),
            pltpu.VMEM((tokens, width), jnp.bfloat16),
            pltpu.VMEM((2 * SUMM, width), jnp.bfloat16),
            pltpu.VMEM((grp_count, ctx_count, 2 * SUMM, width), jnp.bfloat16),
            pltpu.VMEM((all_keys, width), jnp.bfloat16),
            pltpu.VMEM((all_keys, width), jnp.bfloat16),
            pltpu.VMEM((H, tokens, PAIR), jnp.float32),
            pltpu.VMEM((H, tokens, PAIR), jnp.float32),
            pltpu.SemaphoreType.DMA((2 * pairs,)),
            pltpu.SemaphoreType.DMA((2 * pairs,)),
            pltpu.SemaphoreType.DMA((ctx_count,)),
            pltpu.SemaphoreType.DMA((ctx_count,)),
            pltpu.SemaphoreType.DMA((grp_count,)),
            pltpu.SemaphoreType.DMA((grp_count,)),
            pltpu.SemaphoreType.DMA,
            pltpu.SemaphoreType.DMA((4,)),
        ],
        compiler_params=pltpu.CompilerParams(
            collective_id=0, has_side_effects=True, vmem_limit_bytes=56 * 1024 * 1024
        ),
    )(summary_pos[0], queries[0], keys[0], values[0])[None]


def solution(mesh):
    placed = (
        P("grp", "ctx", None),
        P("grp", "ctx", None),
        P("grp", "ctx", None),
        P("grp", "ctx", None),
    )
    return jax.shard_map(
        shards, mesh=mesh, in_specs=placed, out_specs=P("grp", "ctx", None), check_vma=False
    )
```
